32 devices in a mesh: groups: 2 (over y), store: 16 (over z, x, core).
Axes of the slice: x: 2, y: 2, z: 4, core: 2. Of those that a mesh axis runs over, the one named last changes fastest.
Arguments:
- layer_input: bfloat16 [12288, 8192], P('groups', 'store'), parts along dimension 0, may hold values from -6 to 6
- output_grad: bfloat16 [12288, 8192], P('groups', 'store'), parts along dimension 0, may hold values from -6 to 6
- proj_in: bfloat16 [8192, 64], P('store'), may hold values from -0.0625 to 0.0625
- proj_out: bfloat16 [8192, 64], P('store'), may hold values from -0.0625 to 0.0625
- precond_in: float32 [64, 64], replicated
- precond_out: float32 [64, 64], replicated
- query_lengths: int32 [768], P('groups'), parts along dimension 0, may hold values from 1 to 16
- store_rows: bfloat16 [8192, 4096], P('store'), may hold values from -0.0234375 to 0.0234375
- store_live: int32 [16], P('store'), may hold values from 256 to 512, as said below
Outputs:
- scores: float32 [768, 8192], P('groups', 'store'), parts along dimension 0
The draws below stay inside these ranges and needn't reach their ends.
There are 2 independent parts, one for each index of `groups`. The reference program is written for one: setup_inputs(seed, part) draws one part's arguments, and reference() takes and returns one part's arrays. A program takes and returns all parts, laid end to end along the dimension named above; an argument that names none is the same for every part. Nothing has to cross between parts.
Inputs may be any that keep to these rules, and one draw needn't show every extreme that they name: Shard k of the store holds store_live[k] live rows at its head; some shard is full.
All inputs are finite; a program needn't handle non-finite values.
Results may differ from the reference program's by a relative error of at most 0.0029.
Values may be sent and summed in bfloat16 or wider, within the bound.
A program may use at most 128 MiB of HBM per device.

```python
import math
import jax
import jax.numpy as jnp
from jax import lax

D = 8192
RANK = 64
QLEN = 16
QUERIES = 384
STORE_DEV = 512
GW = 4096
TOKQ = 6144
STORE = 8192
N_STORE = 16


def precond_matrix(key):
    diag_key = jax.random.fold_in(key, 1)
    off_key = jax.random.fold_in(key, 2)
    diagonal = jax.random.uniform(diag_key, (RANK,), jnp.float32, 0.5, 2.0)
    spread = jax.random.normal(off_key, (RANK, RANK), jnp.float32) * (0.4 / math.sqrt(RANK))
    return (jnp.diag(diagonal) + spread).astype(jnp.float32)


def draw_precond_in(key, part):
    return precond_matrix(jax.random.fold_in(key, 11))


def draw_precond_out(key, part):
    return precond_matrix(jax.random.fold_in(key, 23))


def draw_store_live(key, part):
    shards = STORE // STORE_DEV
    counts = jax.random.randint(jax.random.fold_in(key, 5), (shards,), STORE_DEV // 2, STORE_DEV + 1)
    full_shard = jax.random.randint(jax.random.fold_in(key, 7), (), 0, shards)
    return jnp.where(jnp.arange(shards) == full_shard, STORE_DEV, counts).astype(jnp.int32)


def touch_ends(entries, key, smallest, high):
    shape = entries.shape
    spot = [jax.random.randint(jax.random.fold_in(key, axis), (), 0, shape[axis]) for axis in range(len(shape))]
    entries = entries.at[tuple(spot)].set(smallest)
    longest = shape.index(max(shape))
    spot[longest] = (spot[longest] + 1) % shape[longest]
    return entries.at[tuple(spot)].set(high)


def level_of(rng, dims, pieces, smallest, largest):
    gain, own = 1.0, jax.random.fold_in(rng, 6)
    for axis_at, blocks in pieces:
        heights = jnp.exp(jax.random.uniform(jax.random.fold_in(own, axis_at), (blocks,), jnp.float32, smallest / len(pieces), largest / len(pieces)))
        gain = gain * jnp.repeat(heights, dims[axis_at] // blocks).reshape([-1 if axis == axis_at else 1 for axis in range(len(dims))])
    return gain


def gaussian(rng, shape, deviation, reach, cuts=(), kind=jnp.bfloat16):
    entries = jax.random.normal(rng, shape, jnp.float32) * deviation
    if len(cuts) > 0:
        entries = level_of(rng, shape, cuts, -0.22, 0.18) * entries
    return jnp.clip(entries, min=-reach, max=reach).astype(kind)


def setup_inputs(seed: int = 0, part: int = 0) -> dict:
    seeds = jax.random.split(jax.random.key(seed), 10)
    part_splits = jax.random.split(jax.random.fold_in(seeds[9], part), 10)
    return {
        "layer_input": gaussian(part_splits[0], (TOKQ, D), 1.0, 6.0, ((1, 16),)),
        "output_grad": gaussian(part_splits[1], (TOKQ, D), 1.0, 6.0, ((1, 16),)),
        "proj_in": gaussian(seeds[2], (D, RANK), D ** -0.5, 0.0625, ((0, 16),)),
        "proj_out": gaussian(seeds[3], (D, RANK), D ** -0.5, 0.0625, ((0, 16),)),
        "precond_in": draw_precond_in(jax.random.fold_in(seeds[9], 71), part),
        "precond_out": draw_precond_out(jax.random.fold_in(seeds[9], 71), part),
        "query_lengths": touch_ends(jax.random.randint(part_splits[6], (QUERIES,), 1, QLEN + 1), jax.random.fold_in(part_splits[6], 1), 1, QLEN).astype(jnp.int32),
        "store_rows": gaussian(seeds[7], (STORE, GW), (1.0 / (4 * RANK)), 0.0234375, ((0, 16),)),
        "store_live": draw_store_live(jax.random.fold_in(seeds[9], 71), part),
    }


def precondition(factors, lengths, precond_in, precond_out):
    query_count = lengths.shape[0]
    proj_rank = precond_in.shape[0]
    query_len = factors.shape[0] // query_count
    token_keep = (jnp.arange(query_len, dtype=jnp.int32)[None, :] < lengths[:, None]).astype(jnp.float32)
    input_side = factors[:, :proj_rank].reshape(query_count, query_len, proj_rank) * token_keep[:, :, None]
    output_side = factors[:, proj_rank:].reshape(query_count, query_len, proj_rank)
    outer_sums = jnp.einsum("qti,qtj->qij", input_side, output_side, precision=lax.Precision.HIGHEST)
    left_side = jnp.einsum("ai,qij->qaj", precond_in, outer_sums, precision=lax.Precision.HIGHEST)
    conditioned = jnp.einsum("qaj,jb->qab", left_side, precond_out, precision=lax.Precision.HIGHEST)
    return conditioned.reshape(query_count, proj_rank * proj_rank).astype(jnp.bfloat16)


def reference(layer_input, output_grad, proj_in, proj_out, precond_in, precond_out, query_lengths, store_rows, store_live):
    input_low = jnp.dot(layer_input, proj_in, preferred_element_type=jnp.float32)
    output_low = jnp.dot(output_grad, proj_out, preferred_element_type=jnp.float32)
    factors = jnp.concatenate([input_low, output_low], axis=1)
    query_grads = precondition(factors, query_lengths, precond_in, precond_out).astype(jnp.float32)
    blocks = store_rows.reshape(N_STORE, STORE_DEV, GW)
    row_index = jnp.arange(STORE_DEV, dtype=jnp.int32)

    def one_block(packed):
        block_rows, live_rows = packed
        products = lax.dot_general(query_grads, block_rows.astype(jnp.float32), (((1,), (1,)), ((), ())), precision=lax.Precision.HIGHEST)
        return jnp.where(row_index[None, :] < live_rows, products, 0.0)

    result = lax.map(one_block, (blocks, store_live))
    return jnp.transpose(result, (1, 0, 2)).reshape(QUERIES, N_STORE * STORE_DEV)
```

```python
import functools

import jax
import jax.numpy as jnp
from jax import lax
from jax.experimental import pallas as pl
from jax.experimental.pallas import tpu as pltpu
from jax.sharding import PartitionSpec as P

STEPS = 512.0
LOW = 40.0
TOP = 32767.0
LOG2E = 1.4426950408889634
TINY = 1e-30
MESH_IDS = pl.DeviceIdType.MESH


def encode(values):
    size = jnp.log(jnp.maximum(jnp.abs(values), TINY)) * (LOG2E * STEPS) + LOW * STEPS
    size = jnp.clip(jnp.floor(size + 0.5), 0.0, TOP)
    return jnp.where(values < 0.0, -size, size).astype(jnp.int32).astype(jnp.int16)


def decode(codes):
    signed = codes.astype(jnp.int32).astype(jnp.float32)
    size = jnp.exp2(jnp.abs(signed) * (1.0 / STEPS) - LOW)
    return jnp.where(signed < 0.0, -size, jnp.where(signed > 0.0, size, 0.0))


def split_store(n):
    cores = 2 if n % 2 == 0 else 1
    rest = n // cores
    xs = 1
    while (2 * xs) ** 3 <= rest and rest % (2 * xs) == 0:
        xs *= 2
    return rest // xs, xs, cores


def pieces_of(rows, wanted):
    count = wanted
    while count > 1 and (rows % count or (rows // count) % 16):
        count -= 1
    return count


def reduce_kernel(
    zs, xs, cs, parts,
    in_hbm, out_hbm, w_in, w_out, full,
    in_rows, out_rows, wide, core_send, core_recv, own, x_send, x_recv, z_send, z_recv,
    load_sem, cs_sem, cr_sem, xs_sem, xr_sem, zs_sem, zr_sem,
    gz_s, gz_r, gx_s, gx_r, gc_s, gc_r,
):
    rank = w_in.shape[1]
    slab = own.shape[1]
    run = slab // zs
    me = lax.axis_index("store")
    c = lax.rem(me, cs)
    x = lax.rem(me // cs, xs)
    z = me // (cs * xs)

    def device(zz, xx, cc):
        return {"store": (zz * xs + xx) * cs + cc}

    def start_of(cc, xx, p):
        return pl.multiple_of(((cc * xs + xx) * parts + p) * slab, slab)

    x_of = [lax.rem(x + d, xs) for d in range(xs)]
    z_of = [lax.rem(z + d, zs) for d in range(zs)]
    core = 1 - c if cs == 2 else c

    order = []
    x_order = list(range(1, xs)) + [0]
    if cs == 2:
        order += [(1, d, p) for p in range(parts) for d in x_order]
    order += [(0, d, p) for p in range(parts) for d in x_order]
    loads = []
    for k, (side, d, p) in enumerate(order):
        rows = pl.ds(start_of(core if side else c, x_of[d], p), slab)
        pair = (
            pltpu.make_async_copy(in_hbm.at[rows], in_rows.at[k], load_sem.at[2 * k]),
            pltpu.make_async_copy(out_hbm.at[rows], out_rows.at[k], load_sem.at[2 * k + 1]),
        )
        for load in pair:
            load.start()
        loads.append(pair)

    barrier = pltpu.get_barrier_semaphore()
    partners = [device(z, x_of[d], c) for d in range(1, xs)]
    partners += [device(z_of[d], x, c) for d in range(1, zs)]
    if cs == 2:
        partners.append(device(z, x, core))
    for partner in partners:
        pl.semaphore_signal(barrier, inc=1, device_id=partner, device_id_type=MESH_IDS)

    wide[...] = jnp.zeros_like(wide)
    wide[0, :, :rank] = w_in[...]
    wide[1, :, rank:] = w_out[...]

    def project(k):
        for load in loads[k]:
            load.wait()
        return jnp.dot(
            in_rows[k], wide[0], preferred_element_type=jnp.float32
        ) + jnp.dot(out_rows[k], wide[1], preferred_element_type=jnp.float32)

    def send(src, dst, s_sem, r_sem, target):
        copy = pltpu.make_async_remote_copy(
            src_ref=src, dst_ref=dst, send_sem=s_sem, recv_sem=r_sem,
            device_id=target, device_id_type=MESH_IDS,
        )
        copy.start()
        return copy

    sent = []
    cores = {}
    first = True
    for k, (side, d, p) in enumerate(order):
        slot = p * xs + d
        if side:
            core_send[slot] = project(k)
            if first:
                pl.semaphore_wait(barrier, len(partners))
                first = False
            cores[slot] = send(
                core_send.at[slot], core_recv.at[slot], cs_sem.at[slot], cr_sem.at[slot],
                device(z, x, core),
            )
            sent.append(cores[slot])
    xcopies = {}
    for k, (side, d, p) in enumerate(order):
        if side:
            continue
        slot = p * xs + d
        total = project(k)
        if first:
            pl.semaphore_wait(barrier, len(partners))
            first = False
        if cs == 2:
            cores[slot].wait_recv()
            total = total + core_recv[slot]
        if d == 0:
            own[p] = total
        else:
            at = p * xs + d
            x_send[at] = encode(total)
            xcopies[p, d] = send(
                x_send.at[at], x_recv.at[at], xs_sem.at[at], xr_sem.at[at], device(z, x_of[d], c)
            )
            sent.append(xcopies[p, d])
    zcopies = {}
    for p in range(parts):
        total = own[p]
        for d in range(1, xs):
            xcopies[p, d].wait_recv()
            total = total + decode(x_recv[p * xs + d])
        own[p] = total
        z_send[p] = encode(total)
        for d in range(1, zs):
            at = p * zs + d
            zcopies[p, d] = send(
                z_send.at[p, pl.ds(pl.multiple_of(z_of[d] * run, run), run)],
                z_recv.at[at], zs_sem.at[at], zr_sem.at[at], device(z_of[d], x, c),
            )
            sent.append(zcopies[p, d])
    gz = {}
    for p in range(parts):
        total = own[p, pl.ds(pl.multiple_of(z * run, run), run), :]
        for d in range(1, zs):
            zcopies[p, d].wait_recv()
            total = total + decode(z_recv[p * zs + d])
        mine = pl.ds(pl.multiple_of(start_of(c, x, p) + z * run, run), run)
        full[mine, :] = encode(total)
        for d in range(1, zs):
            at = p * zs + d
            gz[p, d] = send(
                full.at[mine], full.at[mine], gz_s.at[at], gz_r.at[at], device(z_of[d], x, c)
            )
            sent.append(gz[p, d])
    gx = {}
    gc = {}
    for p in range(parts):
        for d in range(1, zs):
            gz[p, d].wait_recv()
        mine = pl.ds(start_of(c, x, p), slab)
        for d in range(1, xs):
            at = p * xs + d
            gx[p, d] = send(
                full.at[mine], full.at[mine], gx_s.at[at], gx_r.at[at], device(z, x_of[d], c)
            )
            sent.append(gx[p, d])
        if cs == 2:
            at = p * xs
            gc[at] = send(
                full.at[mine], full.at[mine], gc_s.at[at], gc_r.at[at], device(z, x, core)
            )
            sent.append(gc[at])
    for p in range(parts):
        for d in range(1, xs):
            gx[p, d].wait_recv()
            if cs == 2:
                at = p * xs + d
                came = pl.ds(start_of(c, lax.rem(x + xs - d, xs), p), slab)
                gc[at] = send(
                    full.at[came], full.at[came], gc_s.at[at], gc_r.at[at], device(z, x, core)
                )
                sent.append(gc[at])
    for copy in gc.values():
        copy.wait_recv()
    for copy in sent:
        copy.wait_send()


def reduced_factors(n, layer_input, output_grad, proj_in, proj_out):
    zs, xs, cs = split_store(n)
    tokens, depth = layer_input.shape
    width = 2 * proj_in.shape[1]
    parts = pieces_of(tokens // n, 2)
    slab = tokens // (cs * xs * parts)
    run = slab // zs
    slabs = cs * xs * parts
    dma = pltpu.SemaphoreType.DMA
    return pl.pallas_call(
        functools.partial(reduce_kernel, zs, xs, cs, parts),
        out_shape=jax.ShapeDtypeStruct((tokens, width), jnp.int16),
        in_specs=[pl.BlockSpec(memory_space=pl.ANY)] * 2
        + [pl.BlockSpec(memory_space=pltpu.VMEM)] * 2,
        out_specs=pl.BlockSpec(memory_space=pltpu.VMEM),
        scratch_shapes=[
            pltpu.VMEM((slabs, slab, depth), jnp.bfloat16),
            pltpu.VMEM((slabs, slab, depth), jnp.bfloat16),
            pltpu.VMEM((2, depth, width), jnp.bfloat16),
            pltpu.VMEM((parts * xs, slab, width), jnp.float32),
            pltpu.VMEM((parts * xs, slab, width), jnp.float32),
            pltpu.VMEM((parts, slab, width), jnp.float32),
            pltpu.VMEM((parts * xs, slab, width), jnp.int16),
            pltpu.VMEM((parts * xs, slab, width), jnp.int16),
            pltpu.VMEM((parts, slab, width), jnp.int16),
            pltpu.VMEM((parts * zs, run, width), jnp.int16),
            dma((2 * slabs,)),
            dma((parts * xs,)), dma((parts * xs,)),
            dma((parts * xs,)), dma((parts * xs,)),
            dma((parts * zs,)), dma((parts * zs,)),
            dma((parts * zs,)), dma((parts * zs,)),
            dma((parts * xs,)), dma((parts * xs,)),
            dma((parts * xs,)), dma((parts * xs,)),
        ],
        compiler_params=pltpu.CompilerParams(
            collective_id=0, has_side_effects=True, vmem_limit_bytes=48 * 1024 * 1024
        ),
        name="reduce_factors",
    )(layer_input, output_grad, proj_in, proj_out)


def halves(values):
    high = values.astype(jnp.bfloat16)
    return high, (values - high.astype(jnp.float32)).astype(jnp.bfloat16)


def score_kernel(
    query_len, factors, pin, pout, lengths, live, store_hbm, scores,
    store, grads, corner, store_sem,
):
    rank = pin.shape[0]
    width = 2 * rank
    queries = lengths.shape[0]
    group = 8
    tokens = group * query_len
    fetch = pltpu.make_async_copy(store_hbm, store, store_sem)
    fetch.start()

    corner[...] = jnp.zeros_like(corner)
    corner[:rank, :rank] = pin[...]
    flipped = corner[...].T
    corner[:rank, :rank] = jnp.zeros_like(pin)
    corner[rank:, rank:] = pout[...]
    w_high, w_low = halves(flipped + corner[...])
    weights = jnp.concatenate([w_high, w_low], axis=1)
    weights = jnp.concatenate([weights, weights], axis=0)

    lane = lax.broadcasted_iota(jnp.int32, (group, tokens), 1)
    row = lax.broadcasted_iota(jnp.int32, (group, tokens), 0)
    token = lane - row * query_len
    low_lane = lax.broadcasted_iota(jnp.int32, (1, 1, width), 2) < rank

    def one_group(first):
        part = decode(factors[pl.ds(first * query_len, tokens), :])
        high, low = halves(part)
        both = jnp.dot(
            jnp.concatenate([high, low], axis=1), weights, preferred_element_type=jnp.float32
        )
        done = both[:, :width] + both[:, width:]
        left = done.T[:rank]
        keep = (token >= 0) & (token < lengths[pl.ds(first, group), :])
        left_high = left.astype(jnp.bfloat16).astype(jnp.float32)
        left_low = left - left_high
        spread = [
            jnp.where(keep[None], side[:, None, :], 0.0)
            .reshape(rank * group, tokens)
            .astype(jnp.bfloat16)
            for side in (left_high, left_low)
        ]
        right = done[:, rank:]
        right_high, right_low = halves(jnp.concatenate([right, right], axis=1))
        column = jnp.concatenate([right_high, right_low], axis=1)
        outer = jnp.dot(
            jnp.concatenate(spread, axis=1),
            jnp.concatenate([column, column], axis=0),
            preferred_element_type=jnp.float32,
        )
        outer = (outer[:, :width] + outer[:, width:]).reshape(rank // 2, 2, group, width)
        return jnp.where(low_lane, outer[:, 0], outer[:, 1])

    def body(step, carry):
        first = pl.multiple_of(step * 2 * group, 2 * group)
        pair = jnp.concatenate([one_group(first), one_group(first + group)], axis=1)
        pair = pair.astype(jnp.bfloat16)
        for m in range(rank // 2):
            grads[pl.ds(first, 2 * group), m * width : (m + 1) * width] = pair[m]
        return carry

    lax.fori_loop(0, queries // (2 * group), body, 0)

    fetch.wait()
    tile = 256
    for at in range(0, store.shape[0], tile):
        products = lax.dot_general(
            grads[...], store[at : at + tile, :], (((1,), (1,)), ((), ())),
            preferred_element_type=jnp.float32,
        )
        index = lax.broadcasted_iota(jnp.int32, (1, tile), 1) + at
        scores[:, at : at + tile] = jnp.where(index < live[0], products, 0.0)


def score(factors, precond_in, precond_out, lengths, store_rows, store_live):
    queries = lengths.shape[0]
    query_len = factors.shape[0] // queries
    rank = precond_in.shape[0]
    rows, flat = store_rows.shape
    vmem = pl.BlockSpec(memory_space=pltpu.VMEM)
    return pl.pallas_call(
        functools.partial(score_kernel, query_len),
        out_shape=jax.ShapeDtypeStruct((queries, rows), jnp.float32),
        in_specs=[vmem, vmem, vmem, vmem, pl.BlockSpec(memory_space=pltpu.SMEM),
                  pl.BlockSpec(memory_space=pl.ANY)],
        out_specs=vmem,
        scratch_shapes=[
            pltpu.VMEM((rows, flat), jnp.bfloat16),
            pltpu.VMEM((queries, flat), jnp.bfloat16),
            pltpu.VMEM((2 * rank, 2 * rank), jnp.float32),
            pltpu.SemaphoreType.DMA,
        ],
        compiler_params=pltpu.CompilerParams(vmem_limit_bytes=48 * 1024 * 1024),
        name="score_store",
    )(factors, precond_in, precond_out, lengths[:, None], store_live, store_rows)


def solution(mesh):
    n = mesh.shape["store"]

    def local(
        layer_input, output_grad, proj_in, proj_out, precond_in, precond_out,
        query_lengths, store_rows, store_live,
    ):
        factors = reduced_factors(n, layer_input, output_grad, proj_in, proj_out)
        return score(factors, precond_in, precond_out, query_lengths, store_rows, store_live)

    placed = (
        P("groups", "store"),
        P("groups", "store"),
        P("store", None),
        P("store", None),
        P(),
        P(),
        P("groups"),
        P("store", None),
        P("store"),
    )
    return jax.shard_map(
        local, mesh=mesh, in_specs=placed, out_specs=P("groups", "store"), check_vma=False
    )
```

```python
import functools

import jax
import jax.numpy as jnp
from jax import lax
from jax.experimental import pallas as pl
from jax.experimental.pallas import tpu as pltpu
from jax.sharding import PartitionSpec as P

STEPS = 512.0
LOW = 40.0
TOP = 32767.0
LOG2E = 1.4426950408889634
TINY = 1e-30
MESH_IDS = pl.DeviceIdType.MESH
NT = (((1,), (1,)), ((), ()))
PARTS = 3


def encode(values):
    size = jnp.log(jnp.maximum(jnp.abs(values), TINY)) * (LOG2E * STEPS) + LOW * STEPS
    size = jnp.clip(jnp.floor(size + 0.5), 0.0, TOP)
    return jnp.where(values < 0.0, -size, size).astype(jnp.int32).astype(jnp.int16)


def decode(codes):
    signed = codes.astype(jnp.int32).astype(jnp.float32)
    size = jnp.exp2(jnp.abs(signed) * (1.0 / STEPS) - LOW)
    return jnp.where(signed < 0.0, -size, jnp.where(signed > 0.0, size, 0.0))


def split_store(n):
    cores = 2 if n % 2 == 0 else 1
    rest = n // cores
    xs = 1
    while (2 * xs) ** 3 <= rest and rest % (2 * xs) == 0:
        xs *= 2
    return rest // xs, xs, cores


def pieces_of(rows, slab, block, wanted):
    count = wanted
    while count > 1 and (rows % count or (rows // count) % 16 or (slab // count) % block):
        count -= 1
    return count


def halves(values):
    high = values.astype(jnp.bfloat16)
    return high, (values - high.astype(jnp.float32)).astype(jnp.bfloat16)


def lanes_to_rows(row, lanes):
    return jnp.broadcast_to(row, (lanes, lanes)).T


def attribution_kernel(
    zs, xs, cs, parts, query_len,
    in_hbm, out_hbm, w_in, w_out, pin, pout, lengths, live, store_hbm, scores,
    full, store, grads, corner, counted, weights, left_parts, right_parts, store_sem,
    in_rows, out_rows, wide, core_send, core_recv, own, x_send, x_recv, z_send, z_recv,
    load_sem, cs_sem, cr_sem, xs_sem, xr_sem, zs_sem, zr_sem,
    gz_s, gz_r, gx_s, gx_r, gc_s, gc_r,
):
    rank = w_in.shape[0]
    width = 2 * rank
    group = 8
    tokens = group * query_len
    slab = own.shape[1]
    run = slab // zs
    me = lax.axis_index("store")
    c = lax.rem(me, cs)
    x = lax.rem(me // cs, xs)
    z = me // (cs * xs)

    def device(zz, xx, cc):
        return {"store": (zz * xs + xx) * cs + cc}

    def start_of(cc, xx, p):
        return pl.multiple_of(((cc * xs + xx) * parts + p) * slab, slab)

    x_of = [lax.rem(x + d, xs) for d in range(xs)]
    z_of = [lax.rem(z + d, zs) for d in range(zs)]
    core = 1 - c if cs == 2 else c

    order = []
    x_order = list(range(1, xs)) + [0]
    if cs == 2:
        order += [(1, d, p) for p in range(parts) for d in x_order]
    order += [(0, d, p) for p in range(parts) for d in x_order]
    loads = []
    for k, (side, d, p) in enumerate(order):
        rows = pl.ds(start_of(core if side else c, x_of[d], p), slab)
        pair = (
            pltpu.make_async_copy(in_hbm.at[rows], in_rows.at[k], load_sem.at[2 * k]),
            pltpu.make_async_copy(out_hbm.at[rows], out_rows.at[k], load_sem.at[2 * k + 1]),
        )
        for load in pair:
            load.start()
        loads.append(pair)

    fetch = pltpu.make_async_copy(store_hbm, store, store_sem)
    fetch.start()

    barrier = pltpu.get_barrier_semaphore()
    partners = [device(z, x_of[d], c) for d in range(1, xs)]
    partners += [device(z_of[d], x, c) for d in range(1, zs)]
    if cs == 2:
        partners.append(device(z, x, core))
    for partner in partners:
        pl.semaphore_signal(barrier, inc=1, device_id=partner, device_id_type=MESH_IDS)

    wide[...] = jnp.zeros_like(wide)
    wide[0, :rank, :] = w_in[...]
    wide[1, rank:, :] = w_out[...]

    def project(k):
        for load in loads[k]:
            load.wait()
        return lax.dot_general(
            in_rows[k], wide[0], NT, preferred_element_type=jnp.float32
        ) + lax.dot_general(out_rows[k], wide[1], NT, preferred_element_type=jnp.float32)

    def send(src, dst, s_sem, r_sem, target):
        copy = pltpu.make_async_remote_copy(
            src_ref=src, dst_ref=dst, send_sem=s_sem, recv_sem=r_sem,
            device_id=target, device_id_type=MESH_IDS,
        )
        copy.start()
        return copy

    sent = []
    cores = {}
    first = True
    for k, (side, d, p) in enumerate(order):
        slot = p * xs + d
        if side:
            core_send[slot] = project(k)
            if first:
                pl.semaphore_wait(barrier, len(partners))
                first = False
            cores[slot] = send(
                core_send.at[slot], core_recv.at[slot], cs_sem.at[slot], cr_sem.at[slot],
                device(z, x, core),
            )
            sent.append(cores[slot])
    xcopies = {}
    for k, (side, d, p) in enumerate(order):
        if side:
            continue
        slot = p * xs + d
        total = project(k)
        if first:
            pl.semaphore_wait(barrier, len(partners))
            first = False
        if cs == 2:
            cores[slot].wait_recv()
            total = total + core_recv[slot]
        if d == 0:
            own[p] = total
        else:
            at = p * xs + d
            x_send[at] = encode(total)
            xcopies[p, d] = send(
                x_send.at[at], x_recv.at[at], xs_sem.at[at], xr_sem.at[at], device(z, x_of[d], c)
            )
            sent.append(xcopies[p, d])
    corner[...] = jnp.zeros_like(corner)
    corner[:rank, :rank] = pin[...]
    flipped = corner[...].T
    corner[:rank, :rank] = jnp.zeros_like(pin)
    corner[rank:, rank:] = pout[...]
    w_high, w_low = halves(flipped + corner[...])
    both_weights = jnp.concatenate([w_high, w_low], axis=1)
    weights[...] = jnp.concatenate([both_weights, both_weights], axis=0)
    for at in range(0, lengths.shape[1], width):
        counted[at : at + width, :] = lanes_to_rows(
            lengths[:, at : at + width].astype(jnp.float32), width
        )

    zcopies = {}
    for p in range(parts):
        total = own[p]
        for d in range(1, xs):
            xcopies[p, d].wait_recv()
            total = total + decode(x_recv[p * xs + d])
        own[p] = total
        z_send[p] = encode(total)
        for d in range(1, zs):
            at = p * zs + d
            zcopies[p, d] = send(
                z_send.at[p, pl.ds(pl.multiple_of(z_of[d] * run, run), run)],
                z_recv.at[at], zs_sem.at[at], zr_sem.at[at], device(z_of[d], x, c),
            )
            sent.append(zcopies[p, d])
    gz = {}
    for p in range(parts):
        total = own[p, pl.ds(pl.multiple_of(z * run, run), run), :]
        for d in range(1, zs):
            zcopies[p, d].wait_recv()
            total = total + decode(z_recv[p * zs + d])
        mine = pl.ds(pl.multiple_of(start_of(c, x, p) + z * run, run), run)
        full[mine, :] = encode(total)
        for d in range(1, zs):
            at = p * zs + d
            gz[p, d] = send(
                full.at[mine], full.at[mine], gz_s.at[at], gz_r.at[at], device(z_of[d], x, c)
            )
            sent.append(gz[p, d])
    lane = lax.broadcasted_iota(jnp.int32, (group, tokens), 1)
    row = lax.broadcasted_iota(jnp.int32, (group, tokens), 0)
    token = lane - row * query_len
    own_tokens = token >= 0
    token = token.astype(jnp.float32)
    low_lane = lax.broadcasted_iota(jnp.int32, (1, 1, width), 2) < rank

    def one_group(k, first_query):
        keep = own_tokens & (token < counted[pl.ds(first_query, group), :])
        spread = [
            jnp.where(keep[None], left_parts[half, k][:, None, :], 0.0)
            .reshape(rank * group, tokens)
            .astype(jnp.bfloat16)
            for half in range(2)
        ]
        column = right_parts[pl.ds(pl.multiple_of(k * tokens, tokens), tokens), :]
        outer = jnp.dot(
            jnp.concatenate(spread, axis=1),
            jnp.concatenate([column, column], axis=0),
            preferred_element_type=jnp.float32,
        )
        outer = (outer[:, :width] + outer[:, width:]).reshape(rank // 2, 2, group, width)
        return jnp.where(low_lane, outer[:, 0], outer[:, 1])

    def grads_of(start):
        high, low = halves(decode(full[pl.ds(start, slab), :]))
        both = jnp.dot(
            jnp.concatenate([high, low], axis=1), weights[...], preferred_element_type=jnp.float32
        )
        done = both[:, :width] + both[:, width:]
        for k in range(slab // tokens):
            left = done[k * tokens : (k + 1) * tokens].T[:rank]
            left_high = left.astype(jnp.bfloat16).astype(jnp.float32)
            left_parts[0, k] = left_high
            left_parts[1, k] = left - left_high
        right = done[:, rank:]
        right_high, right_low = halves(jnp.concatenate([right, right], axis=1))
        right_parts[...] = jnp.concatenate([right_high, right_low], axis=1)

        def body(step, carry):
            first = pl.multiple_of(start // query_len + step * 2 * group, 2 * group)
            pair = jnp.concatenate(
                [one_group(2 * step, first), one_group(2 * step + 1, first + group)], axis=1
            ).astype(jnp.bfloat16)
            for m in range(rank // 2):
                grads[pl.ds(first, 2 * group), m * width : (m + 1) * width] = pair[m]
            return carry

        lax.fori_loop(0, slab // (2 * tokens), body, 0)

    gx = {}
    gc = {}
    for p in range(parts):
        for d in range(1, zs):
            gz[p, d].wait_recv()
        mine = pl.ds(start_of(c, x, p), slab)
        for d in range(1, xs):
            at = p * xs + d
            gx[p, d] = send(
                full.at[mine], full.at[mine], gx_s.at[at], gx_r.at[at], device(z, x_of[d], c)
            )
            sent.append(gx[p, d])
        if cs == 2:
            at = p * xs
            gc[at] = send(
                full.at[mine], full.at[mine], gc_s.at[at], gc_r.at[at], device(z, x, core)
            )
            sent.append(gc[at])
        grads_of(start_of(c, x, p))
    x_from = [lax.rem(x + xs - d, xs) for d in range(xs)]
    for p in range(parts):
        if cs == 2:
            gc[p * xs].wait_recv()
            grads_of(start_of(core, x, p))
        for d in range(1, xs):
            gx[p, d].wait_recv()
            if cs == 2:
                at = p * xs + d
                came = pl.ds(start_of(c, x_from[d], p), slab)
                gc[at] = send(
                    full.at[came], full.at[came], gc_s.at[at], gc_r.at[at], device(z, x, core)
                )
                sent.append(gc[at])
    for p in range(parts):
        for d in range(1, xs):
            grads_of(start_of(c, x_from[d], p))
            if cs == 2:
                gc[p * xs + d].wait_recv()
                grads_of(start_of(core, x_from[d], p))

    fetch.wait()
    tile = 256
    for at in range(0, store.shape[0], tile):
        products = lax.dot_general(
            grads[...], store[at : at + tile, :], NT, preferred_element_type=jnp.float32
        )
        index = lax.broadcasted_iota(jnp.int32, (1, tile), 1) + at
        scores[:, at : at + tile] = jnp.where(index < live[0], products, 0.0)
    for copy in sent:
        copy.wait_send()


def attribution(
    n, layer_input, output_grad, proj_in, proj_out, precond_in, precond_out, lengths, store_rows,
    store_live,
):
    zs, xs, cs = split_store(n)
    tokens, depth = layer_input.shape
    rank = proj_in.shape[1]
    width = 2 * rank
    queries = lengths.shape[0]
    query_len = tokens // queries
    rows, flat = store_rows.shape
    parts = pieces_of(tokens // n, tokens // (cs * xs), 16 * query_len, PARTS)
    slab = tokens // (cs * xs * parts)
    run = slab // zs
    slabs = cs * xs * parts
    group = 8 * query_len
    dma = pltpu.SemaphoreType.DMA
    vmem = pl.BlockSpec(memory_space=pltpu.VMEM)
    hbm = pl.BlockSpec(memory_space=pl.ANY)
    return pl.pallas_call(
        functools.partial(attribution_kernel, zs, xs, cs, parts, query_len),
        out_shape=jax.ShapeDtypeStruct((queries, rows), jnp.float32),
        in_specs=[hbm, hbm, vmem, vmem, vmem, vmem, vmem,
                  pl.BlockSpec(memory_space=pltpu.SMEM), hbm],
        out_specs=vmem,
        scratch_shapes=[
            pltpu.VMEM((tokens, width), jnp.int16),
            pltpu.VMEM((rows, flat), jnp.bfloat16),
            pltpu.VMEM((queries, flat), jnp.bfloat16),
            pltpu.VMEM((width, width), jnp.float32),
            pltpu.VMEM((queries, width), jnp.float32),
            pltpu.VMEM((2 * width, 2 * width), jnp.bfloat16),
            pltpu.VMEM((2, slab // group, rank, group), jnp.float32),
            pltpu.VMEM((slab, 2 * width), jnp.bfloat16),
            pltpu.SemaphoreType.DMA,
            pltpu.VMEM((slabs, slab, depth), jnp.bfloat16),
            pltpu.VMEM((slabs, slab, depth), jnp.bfloat16),
            pltpu.VMEM((2, width, depth), jnp.bfloat16),
            pltpu.VMEM((parts * xs, slab, width), jnp.float32),
            pltpu.VMEM((parts * xs, slab, width), jnp.float32),
            pltpu.VMEM((parts, slab, width), jnp.float32),
            pltpu.VMEM((parts * xs, slab, width), jnp.int16),
            pltpu.VMEM((parts * xs, slab, width), jnp.int16),
            pltpu.VMEM((parts, slab, width), jnp.int16),
            pltpu.VMEM((parts * zs, run, width), jnp.int16),
            dma((2 * slabs,)),
            dma((parts * xs,)), dma((parts * xs,)),
            dma((parts * xs,)), dma((parts * xs,)),
            dma((parts * zs,)), dma((parts * zs,)),
            dma((parts * zs,)), dma((parts * zs,)),
            dma((parts * xs,)), dma((parts * xs,)),
            dma((parts * xs,)), dma((parts * xs,)),
        ],
        compiler_params=pltpu.CompilerParams(
            collective_id=0, has_side_effects=True, vmem_limit_bytes=56 * 1024 * 1024
        ),
        name="attribution",
    )(
        layer_input, output_grad, proj_in.T, proj_out.T, precond_in, precond_out,
        lengths[None, :], store_live, store_rows,
    )


def solution(mesh):
    n = mesh.shape["store"]

    def local(
        layer_input, output_grad, proj_in, proj_out, precond_in, precond_out,
        query_lengths, store_rows, store_live,
    ):
        return attribution(
            n, layer_input, output_grad, proj_in, proj_out, precond_in, precond_out,
            query_lengths, store_rows, store_live,
        )

    placed = (
        P("groups", "store"),
        P("groups", "store"),
        P("store", None),
        P("store", None),
        P(),
        P(),
        P("groups"),
        P("store", None),
        P("store"),
    )
    return jax.shard_map(
        local, mesh=mesh, in_specs=placed, out_specs=P("groups", "store"), check_vma=False
    )
```

```python
import functools

import jax
import jax.numpy as jnp
from jax import lax
from jax.experimental import pallas as pl
from jax.experimental.pallas import tpu as pltpu
from jax.sharding import PartitionSpec as P

STEPS = 512.0
LOW = 40.0
TOP = 32767.0
LOG2E = 1.4426950408889634
TINY = 1e-30
MESH_IDS = pl.DeviceIdType.MESH
NT = (((1,), (1,)), ((), ()))
PARTS = 3


def encode(values):
    size = jnp.log(jnp.maximum(jnp.abs(values), TINY)) * (LOG2E * STEPS) + LOW * STEPS
    size = jnp.clip(jnp.floor(size + 0.5), 0.0, TOP)
    return jnp.where(values < 0.0, -size, size).astype(jnp.int32).astype(jnp.int16)


def decode(codes):
    signed = codes.astype(jnp.int32).astype(jnp.float32)
    size = jnp.exp2(jnp.abs(signed) * (1.0 / STEPS) - LOW)
    return jnp.where(signed < 0.0, -size, jnp.where(signed > 0.0, size, 0.0))


def split_store(n):
    cores = 2 if n % 2 == 0 else 1
    rest = n // cores
    xs = 1
    while (2 * xs) ** 3 <= rest and rest % (2 * xs) == 0:
        xs *= 2
    return rest // xs, xs, cores


def pieces_of(rows, slab, block, wanted):
    count = wanted
    while count > 1 and (rows % count or (rows // count) % 16 or (slab // count) % block):
        count -= 1
    return count


def halves(values):
    high = values.astype(jnp.bfloat16)
    return high, (values - high.astype(jnp.float32)).astype(jnp.bfloat16)


def lanes_to_rows(row, lanes):
    return jnp.broadcast_to(row, (lanes, lanes)).T


def attribution_kernel(
    zs, xs, cs, parts, query_len,
    in_hbm, out_hbm, w_in, w_out, pin, pout, lengths, live, store_hbm, scores,
    full, store, grads, corner, counted, weights, left_parts, right_parts, store_sem,
    in_rows, out_rows, wide, core_send, core_recv, own, x_send, x_recv, z_send, z_recv,
    load_sem, cs_sem, cr_sem, xs_sem, xr_sem, zs_sem, zr_sem,
    gz_s, gz_r, gx_s, gx_r, gc_s, gc_r,
):
    rank = w_in.shape[0]
    width = 2 * rank
    group = 8
    tokens = group * query_len
    slab = own.shape[1]
    run = slab // zs
    me = lax.axis_index("store")
    c = lax.rem(me, cs)
    x = lax.rem(me // cs, xs)
    z = me // (cs * xs)

    def device(zz, xx, cc):
        return {"store": (zz * xs + xx) * cs + cc}

    def start_of(cc, xx, p):
        return pl.multiple_of(((cc * xs + xx) * parts + p) * slab, slab)

    x_of = [lax.rem(x + d, xs) for d in range(xs)]
    z_of = [lax.rem(z + d, zs) for d in range(zs)]
    core = 1 - c if cs == 2 else c

    order = []
    x_order = list(range(1, xs)) + [0]
    for step in range(parts + 1):
        if cs == 2 and step < parts:
            order += [(1, d, step) for d in x_order]
        if step > 0:
            order += [(0, d, step - 1) for d in x_order]
    loads = []
    for k, (side, d, p) in enumerate(order):
        rows = pl.ds(start_of(core if side else c, x_of[d], p), slab)
        pair = (
            pltpu.make_async_copy(in_hbm.at[rows], in_rows.at[k], load_sem.at[2 * k]),
            pltpu.make_async_copy(out_hbm.at[rows], out_rows.at[k], load_sem.at[2 * k + 1]),
        )
        for load in pair:
            load.start()
        loads.append(pair)

    fetch = pltpu.make_async_copy(store_hbm, store, store_sem)
    fetch.start()

    barrier = pltpu.get_barrier_semaphore()
    partners = [device(z, x_of[d], c) for d in range(1, xs)]
    partners += [device(z_of[d], x, c) for d in range(1, zs)]
    if cs == 2:
        partners.append(device(z, x, core))
    for partner in partners:
        pl.semaphore_signal(barrier, inc=1, device_id=partner, device_id_type=MESH_IDS)

    wide[...] = jnp.zeros_like(wide)
    wide[0, :rank, :] = w_in[...]
    wide[1, rank:, :] = w_out[...]

    def project(k):
        for load in loads[k]:
            load.wait()
        return lax.dot_general(
            in_rows[k], wide[0], NT, preferred_element_type=jnp.float32
        ) + lax.dot_general(out_rows[k], wide[1], NT, preferred_element_type=jnp.float32)

    def send(src, dst, s_sem, r_sem, target):
        copy = pltpu.make_async_remote_copy(
            src_ref=src, dst_ref=dst, send_sem=s_sem, recv_sem=r_sem,
            device_id=target, device_id_type=MESH_IDS,
        )
        copy.start()
        return copy

    corner[...] = jnp.zeros_like(corner)
    corner[:rank, :rank] = pin[...]
    flipped = corner[...].T
    corner[:rank, :rank] = jnp.zeros_like(pin)
    corner[rank:, rank:] = pout[...]
    w_high, w_low = halves(flipped + corner[...])
    both_weights = jnp.concatenate([w_high, w_low], axis=1)
    weights[...] = jnp.concatenate([both_weights, both_weights], axis=0)
    for at in range(0, lengths.shape[1], width):
        counted[at : at + width, :] = lanes_to_rows(
            lengths[:, at : at + width].astype(jnp.float32), width
        )

    sent = []
    cores = {}
    xcopies = {}
    zcopies = {}
    gz = {}
    gx = {}
    gc = {}

    def to_core(p):
        for d in x_order:
            slot = p * xs + d
            core_send[slot] = project(order.index((1, d, p)))
            cores[slot] = send(
                core_send.at[slot], core_recv.at[slot], cs_sem.at[slot], cr_sem.at[slot],
                device(z, x, core),
            )
            sent.append(cores[slot])

    def to_x(p):
        for d in x_order:
            at = p * xs + d
            total = project(order.index((0, d, p)))
            if cs == 2:
                cores[at].wait_recv()
                total = total + core_recv[at]
            if d == 0:
                own[p] = total
            else:
                x_send[at] = encode(total)
                xcopies[p, d] = send(
                    x_send.at[at], x_recv.at[at], xs_sem.at[at], xr_sem.at[at],
                    device(z, x_of[d], c),
                )
                sent.append(xcopies[p, d])

    def to_z(p):
        total = own[p]
        for d in range(1, xs):
            xcopies[p, d].wait_recv()
            total = total + decode(x_recv[p * xs + d])
        own[p] = total
        z_send[p] = encode(total)
        for d in range(1, zs):
            at = p * zs + d
            zcopies[p, d] = send(
                z_send.at[p, pl.ds(pl.multiple_of(z_of[d] * run, run), run)],
                z_recv.at[at], zs_sem.at[at], zr_sem.at[at], device(z_of[d], x, c),
            )
            sent.append(zcopies[p, d])

    def back_z(p):
        total = own[p, pl.ds(pl.multiple_of(z * run, run), run), :]
        for d in range(1, zs):
            zcopies[p, d].wait_recv()
            total = total + decode(z_recv[p * zs + d])
        mine = pl.ds(pl.multiple_of(start_of(c, x, p) + z * run, run), run)
        full[mine, :] = encode(total)
        for d in range(1, zs):
            at = p * zs + d
            gz[p, d] = send(
                full.at[mine], full.at[mine], gz_s.at[at], gz_r.at[at], device(z_of[d], x, c)
            )
            sent.append(gz[p, d])

    lane = lax.broadcasted_iota(jnp.int32, (group, tokens), 1)
    row = lax.broadcasted_iota(jnp.int32, (group, tokens), 0)
    token = lane - row * query_len
    own_tokens = token >= 0
    token = token.astype(jnp.float32)
    low_lane = lax.broadcasted_iota(jnp.int32, (1, 1, width), 2) < rank

    def one_group(k, first_query):
        keep = own_tokens & (token < counted[pl.ds(first_query, group), :])
        spread = [
            jnp.where(keep[None], left_parts[half, k][:, None, :], 0.0)
            .reshape(rank * group, tokens)
            .astype(jnp.bfloat16)
            for half in range(2)
        ]
        column = right_parts[pl.ds(pl.multiple_of(k * tokens, tokens), tokens), :]
        outer = jnp.dot(
            jnp.concatenate(spread, axis=1),
            jnp.concatenate([column, column], axis=0),
            preferred_element_type=jnp.float32,
        )
        outer = (outer[:, :width] + outer[:, width:]).reshape(rank // 2, 2, group, width)
        return jnp.where(low_lane, outer[:, 0], outer[:, 1])

    def grads_of(start):
        high, low = halves(decode(full[pl.ds(start, slab), :]))
        both = jnp.dot(
            jnp.concatenate([high, low], axis=1), weights[...], preferred_element_type=jnp.float32
        )
        done = both[:, :width] + both[:, width:]
        for k in range(slab // tokens):
            left = done[k * tokens : (k + 1) * tokens].T[:rank]
            left_high = left.astype(jnp.bfloat16).astype(jnp.float32)
            left_parts[0, k] = left_high
            left_parts[1, k] = left - left_high
        right = done[:, rank:]
        right_high, right_low = halves(jnp.concatenate([right, right], axis=1))
        right_parts[...] = jnp.concatenate([right_high, right_low], axis=1)

        def body(step, carry):
            first = pl.multiple_of(start // query_len + step * 2 * group, 2 * group)
            pair = jnp.concatenate(
                [one_group(2 * step, first), one_group(2 * step + 1, first + group)], axis=1
            ).astype(jnp.bfloat16)
            for m in range(rank // 2):
                grads[pl.ds(first, 2 * group), m * width : (m + 1) * width] = pair[m]
            return carry

        lax.fori_loop(0, slab // (2 * tokens), body, 0)

    def back_x(p):
        for d in range(1, zs):
            gz[p, d].wait_recv()
        mine = pl.ds(start_of(c, x, p), slab)
        for d in range(1, xs):
            at = p * xs + d
            gx[p, d] = send(
                full.at[mine], full.at[mine], gx_s.at[at], gx_r.at[at], device(z, x_of[d], c)
            )
            sent.append(gx[p, d])
        if cs == 2:
            at = p * xs
            gc[at] = send(
                full.at[mine], full.at[mine], gc_s.at[at], gc_r.at[at], device(z, x, core)
            )
            sent.append(gc[at])
        grads_of(start_of(c, x, p))

    levels = ([to_core] if cs == 2 else []) + [to_x, to_z, back_z, back_x]
    pl.semaphore_wait(barrier, len(partners))
    for step in range(parts + len(levels) - 1):
        for level, act in enumerate(levels):
            if 0 <= step - level < parts:
                act(step - level)
    x_from = [lax.rem(x + xs - d, xs) for d in range(xs)]
    for p in range(parts):
        if cs == 2:
            gc[p * xs].wait_recv()
            grads_of(start_of(core, x, p))
        for d in range(1, xs):
            gx[p, d].wait_recv()
            if cs == 2:
                at = p * xs + d
                came = pl.ds(start_of(c, x_from[d], p), slab)
                gc[at] = send(
                    full.at[came], full.at[came], gc_s.at[at], gc_r.at[at], device(z, x, core)
                )
                sent.append(gc[at])
    for p in range(parts):
        for d in range(1, xs):
            grads_of(start_of(c, x_from[d], p))
            if cs == 2:
                gc[p * xs + d].wait_recv()
                grads_of(start_of(core, x_from[d], p))

    fetch.wait()
    tile = 256
    for at in range(0, store.shape[0], tile):
        products = lax.dot_general(
            grads[...], store[at : at + tile, :], NT, preferred_element_type=jnp.float32
        )
        index = lax.broadcasted_iota(jnp.int32, (1, tile), 1) + at
        scores[:, at : at + tile] = jnp.where(index < live[0], products, 0.0)
    for copy in sent:
        copy.wait_send()


def attribution(
    n, layer_input, output_grad, proj_in, proj_out, precond_in, precond_out, lengths, store_rows,
    store_live,
):
    zs, xs, cs = split_store(n)
    tokens, depth = layer_input.shape
    rank = proj_in.shape[1]
    width = 2 * rank
    queries = lengths.shape[0]
    query_len = tokens // queries
    rows, flat = store_rows.shape
    parts = pieces_of(tokens // n, tokens // (cs * xs), 16 * query_len, PARTS)
    slab = tokens // (cs * xs * parts)
    run = slab // zs
    slabs = cs * xs * parts
    group = 8 * query_len
    dma = pltpu.SemaphoreType.DMA
    vmem = pl.BlockSpec(memory_space=pltpu.VMEM)
    hbm = pl.BlockSpec(memory_space=pl.ANY)
    return pl.pallas_call(
        functools.partial(attribution_kernel, zs, xs, cs, parts, query_len),
        out_shape=jax.ShapeDtypeStruct((queries, rows), jnp.float32),
        in_specs=[hbm, hbm, vmem, vmem, vmem, vmem, vmem,
                  pl.BlockSpec(memory_space=pltpu.SMEM), hbm],
        out_specs=vmem,
        scratch_shapes=[
            pltpu.VMEM((tokens, width), jnp.int16),
            pltpu.VMEM((rows, flat), jnp.bfloat16),
            pltpu.VMEM((queries, flat), jnp.bfloat16),
            pltpu.VMEM((width, width), jnp.float32),
            pltpu.VMEM((queries, width), jnp.float32),
            pltpu.VMEM((2 * width, 2 * width), jnp.bfloat16),
            pltpu.VMEM((2, slab // group, rank, group), jnp.float32),
            pltpu.VMEM((slab, 2 * width), jnp.bfloat16),
            pltpu.SemaphoreType.DMA,
            pltpu.VMEM((slabs, slab, depth), jnp.bfloat16),
            pltpu.VMEM((slabs, slab, depth), jnp.bfloat16),
            pltpu.VMEM((2, width, depth), jnp.bfloat16),
            pltpu.VMEM((parts * xs, slab, width), jnp.float32),
            pltpu.VMEM((parts * xs, slab, width), jnp.float32),
            pltpu.VMEM((parts, slab, width), jnp.float32),
            pltpu.VMEM((parts * xs, slab, width), jnp.int16),
            pltpu.VMEM((parts * xs, slab, width), jnp.int16),
            pltpu.VMEM((parts, slab, width), jnp.int16),
            pltpu.VMEM((parts * zs, run, width), jnp.int16),
            dma((2 * slabs,)),
            dma((parts * xs,)), dma((parts * xs,)),
            dma((parts * xs,)), dma((parts * xs,)),
            dma((parts * zs,)), dma((parts * zs,)),
            dma((parts * zs,)), dma((parts * zs,)),
            dma((parts * xs,)), dma((parts * xs,)),
            dma((parts * xs,)), dma((parts * xs,)),
        ],
        compiler_params=pltpu.CompilerParams(
            collective_id=0, has_side_effects=True, vmem_limit_bytes=56 * 1024 * 1024
        ),
        name="attribution",
    )(
        layer_input, output_grad, proj_in.T, proj_out.T, precond_in, precond_out,
        lengths[None, :], store_live, store_rows,
    )


def solution(mesh):
    n = mesh.shape["store"]

    def local(
        layer_input, output_grad, proj_in, proj_out, precond_in, precond_out,
        query_lengths, store_rows, store_live,
    ):
        return attribution(
            n, layer_input, output_grad, proj_in, proj_out, precond_in, precond_out,
            query_lengths, store_rows, store_live,
        )

    placed = (
        P("groups", "store"),
        P("groups", "store"),
        P("store", None),
        P("store", None),
        P(),
        P(),
        P("groups"),
        P("store", None),
        P("store"),
    )
    return jax.shard_map(
        local, mesh=mesh, in_specs=placed, out_specs=P("groups", "store"), check_vma=False
    )
```
